32 devices in a mesh: parts: 2 (over x), row: 16 (over z, y, core).
Axes of the slice: x: 2, y: 2, z: 4, core: 2. Of those that a mesh axis runs over, the one named last changes fastest.
Arguments:
- basis_values: float32 [32768, 512], P(('parts', 'row')), parts along dimension 0, may hold values from 0.01 to 0.1
- basis_grads: float32 [3, 32768, 512], P(None, ('parts', 'row')), parts along dimension 1, may hold values from -6 to 6
- weights: float32 [32768], P(('parts', 'row')), parts along dimension 0, may hold values from 0.2 to 2
- tile_lists: int32 [32, 8], P('parts'), parts along dimension 0, may hold values from 0 to 15, as said below
- tile_counts: int32 [32], P('parts'), parts along dimension 0, may hold values from 7 to 8, as said below
- owned_rows: int32 [32], P('parts'), parts along dimension 0, may hold values from 0 to 15, as said below
- density_slabs: float32 [2048, 1024], P(('parts', 'row')), parts along dimension 0, as said below
Outputs:
- potential_slabs: float32 [2048, 1024], P(('parts', 'row')), parts along dimension 0
The draws below stay inside these ranges and needn't reach their ends.
There are 2 independent parts, one for each index of `parts`. The reference program is written for one: setup_inputs(seed, part) draws one part's arguments, and reference() takes and returns one part's arrays. A program takes and returns all parts, laid end to end along the dimension named above; each array names one. Nothing has to cross between parts.
Inputs may be any that keep to these rules, and one draw needn't show every extreme that they name: `tile_lists`: each row lists 8 distinct tile indices. `tile_counts`: some batch has all 8 slots significant. `owned_rows`: a permutation of the tile rows. `density_slabs`: the matrix P assembled from the blocks is symmetric, with positive entries.
All inputs are finite; a program needn't handle non-finite values.
Results may differ from the reference program's by a relative error of at most 0.0003.
Values sent between devices are 32-bit elements; how exact they have to be, the bound alone decides.
A program may use at most 128 MiB of HBM per device.

```python
import math
import jax
import jax.numpy as jnp
from jax import lax

TS = 64
NPTS = 1024
K = 8
FUNCS = 512
NT = 16
N_ROW = 16


def row_order(key):
    return jax.random.permutation(key, NT).astype(jnp.int32)


def draw_owned_rows(key, part):
    return row_order(key)


def draw_density_slabs(key, part):
    order = row_order(key)
    key = jax.random.fold_in(key, 11)
    width = NT * TS
    base = jax.random.uniform(key, (width, width), jnp.float32)
    sym = 0.5 * (base + base.T)
    full = 0.0002 + 0.002 * sym
    return full.reshape(NT, TS, width)[order].reshape(N_ROW * TS, width)


def draw_tile_lists(key, part):
    key = jax.random.fold_in(key, 23)
    keys = jax.random.split(key, N_ROW)
    return jax.vmap(lambda k: jax.random.permutation(k, NT)[:K])(keys).astype(jnp.int32)


def draw_tile_counts(key, part):
    key = jax.random.fold_in(key, 37)
    first, second = jax.random.split(key)
    counts = jax.random.randint(first, (N_ROW,), K - K // 8, K + 1)
    top = jax.random.randint(second, (), 0, N_ROW)
    return counts.at[top].set(K).astype(jnp.int32)


def block_scale(own_key, extent, cuts, smallest, high):
    def one(position, blocks):
        steps = jax.random.uniform(jax.random.fold_in(jax.random.fold_in(own_key, 6), position), (blocks,), jnp.float32, smallest / len(cuts), high / len(cuts))
        return jnp.repeat(jnp.exp(steps), extent[position] // blocks).reshape((-1,) + (1,) * (len(extent) - position - 1))

    gain = one(*cuts[0])
    for cut in cuts[1:]:
        gain = gain * one(*cut)
    return gain


def bell_draw(stream_key, dims, deviation, limit, cuts=(), kind=jnp.bfloat16):
    entries = deviation * jax.random.normal(stream_key, dims, jnp.float32)
    if cuts:
        entries = entries * block_scale(stream_key, dims, cuts, -0.22, 0.18)
    return jnp.clip(entries, -limit, limit).astype(kind)


def setup_inputs(seed: int = 0, part: int = 0) -> dict:
    key_list = jax.random.split(jax.random.key(seed), 8)
    part_splits = jax.random.split(jax.random.fold_in(key_list[7], part), 8)
    basis_values = jnp.clip(jnp.exp(math.log(0.1) - 2.3025851 * jax.random.uniform(part_splits[0], (N_ROW * NPTS, FUNCS), jnp.float32) ** block_scale(part_splits[0], (N_ROW * NPTS, FUNCS), ((0, 16),), -0.2, 0.2)), 0.01, 0.1)
    basis_grads = bell_draw(part_splits[1], (3, N_ROW * NPTS, FUNCS), 1.0, 6.0, ((1, 16),), jnp.float32)
    weights = jnp.clip(jnp.exp(math.log(2.0) - 2.3025851 * jax.random.uniform(part_splits[2], (N_ROW * NPTS,), jnp.float32) ** block_scale(part_splits[2], (N_ROW * NPTS,), ((0, 16),), -0.2, 0.2)), 0.2, 2.0)
    tile_lists = draw_tile_lists(jax.random.fold_in(jax.random.fold_in(key_list[7], part), 71), part)
    tile_counts = draw_tile_counts(jax.random.fold_in(jax.random.fold_in(key_list[7], part), 71), part)
    owned_rows = draw_owned_rows(jax.random.fold_in(jax.random.fold_in(key_list[7], part), 71), part)
    density_slabs = draw_density_slabs(jax.random.fold_in(jax.random.fold_in(key_list[7], part), 71), part)
    return dict(basis_values=basis_values, basis_grads=basis_grads, weights=weights, tile_lists=tile_lists, tile_counts=tile_counts, owned_rows=owned_rows, density_slabs=density_slabs)


KAPPA = 0.804
MU_COEF = 0.2195

def energy_density(rho, sigma):
    coef = 0.75 * (3.0 / math.pi) ** (1.0 / 3.0)
    scale = 4.0 * (3.0 * math.pi ** 2) ** (2.0 / 3.0)
    reduced = sigma / (scale * jnp.power(rho, 8.0 / 3.0))
    factor = 1.0 + KAPPA - KAPPA / (1.0 + MU_COEF * reduced / KAPPA)
    return -coef * jnp.power(rho, 4.0 / 3.0) * factor

def pbe_block(values, grads, wts, dens):
    highest = lax.Precision.HIGHEST
    mixed = jnp.dot(values, dens, precision=highest, preferred_element_type=jnp.float32)
    rho = lax.optimization_barrier(jnp.sum(mixed * values, axis=1))
    slope = 2.0 * lax.optimization_barrier(jnp.sum(mixed[None, :, :] * grads, axis=2))
    sigma = lax.optimization_barrier(jnp.sum(slope * slope, axis=0))
    energy, pull = jax.vjp(energy_density, rho, sigma)
    vrho, vsigma = pull(jnp.ones_like(energy))
    along = lax.optimization_barrier(jnp.sum(slope[:, :, None] * grads, axis=0))
    zeta = wts[:, None] * (0.5 * vrho[:, None] * values + 2.0 * vsigma[:, None] * along)
    return lax.dot_general(values, zeta, (((0,), (0,)), ((), ())), precision=highest, preferred_element_type=jnp.float32)

def reference(basis_values, basis_grads, weights, tile_lists, tile_counts, owned_rows, density_slabs):
    width = NT * TS
    funcs = K * TS
    dens_tiles = jnp.zeros((NT, TS, width), jnp.float32).at[owned_rows].set(density_slabs.reshape(N_ROW, TS, width))
    dens_four = dens_tiles.reshape(NT, TS, NT, TS)
    values_all = basis_values.reshape(N_ROW, NPTS, funcs)
    grads_all = jnp.transpose(basis_grads.reshape(3, N_ROW, NPTS, funcs), (1, 0, 2, 3))
    weights_all = weights.reshape(N_ROW, NPTS)

    def one_batch(carry, item):
        values, grads, wts, listed, count = item
        used = (jnp.arange(K, dtype=jnp.int32) < count).astype(jnp.float32)
        block = dens_four[listed[:, None], :, listed[None, :], :]
        block = block * used[:, None, None, None] * used[None, :, None, None]
        dens = jnp.transpose(block, (0, 2, 1, 3)).reshape(funcs, funcs)
        piece = pbe_block(values, grads, wts, dens)
        mask = jnp.repeat(used, TS)
        piece = piece * mask[:, None] * mask[None, :]
        piece_four = jnp.transpose(piece.reshape(K, TS, K, TS), (0, 2, 1, 3))
        carry = carry.at[listed[:, None], :, listed[None, :], :].add(piece_four)
        return (carry, None)
    start = jnp.zeros((NT, TS, NT, TS), jnp.float32)
    total, _ = lax.scan(one_batch, start, (values_all, grads_all, weights_all, tile_lists, tile_counts))
    full = total.reshape(width, width)
    sym = full + full.T
    return sym.reshape(NT, TS, width)[owned_rows].reshape(N_ROW * TS, width)
```

```python
import functools
import math

import jax
import jax.numpy as jnp
from jax import lax
from jax.experimental import pallas as pl
from jax.experimental.pallas import tpu as pltpu
from jax.sharding import PartitionSpec as P

KAPPA = 0.804
MU_COEF = 0.2195
COEF = 0.75 * (3.0 / math.pi) ** (1.0 / 3.0)
SCALE = 4.0 * (3.0 * math.pi**2) ** (2.0 / 3.0)
MESH = pl.DeviceIdType.MESH
VMEM_LIMIT = 60 * 1024 * 1024
F32, BF16 = jnp.float32, jnp.bfloat16


def pair(load, first, second, tile):
    left, right = load(lax.div(first, 2)), load(lax.div(second, 2))
    low = lax.broadcasted_iota(jnp.int32, left.shape, 1) < tile
    odd = jnp.full(left.shape, lax.rem(first, 2), jnp.int32) == 1
    even = jnp.full(left.shape, lax.rem(second, 2), jnp.int32) == 0
    left = jnp.where(odd, pltpu.roll(left, tile, 1), left)
    right = jnp.where(even, pltpu.roll(right, tile, 1), right)
    return jnp.where(low, left, right)


def place(n):
    me = lax.axis_index("row")
    return me, me // 4, (me // 2) % 2, me % 2


def to(row):
    return {"row": row}


def greet(planes, me, z, y, c):
    barrier = pltpu.get_barrier_semaphore()
    for ok, peer in neighbours(planes, me, z, y, c):
        @pl.when(ok)
        def _():
            pl.semaphore_signal(barrier, inc=1, device_id=to(peer), device_id_type=MESH)
    peers = 2 + (z > 0).astype(jnp.int32) + (z < planes - 1).astype(jnp.int32)
    pl.semaphore_wait(barrier, peers)


def neighbours(planes, me, z, y, c):
    return (
        (z >= 0, me + 1 - 2 * c),
        (z >= 0, me + 2 - 4 * y),
        (z > 0, me - 4),
        (z < planes - 1, me + 4),
    )


def pack_kernel(n, slab_ref, owned_ref, own_ref):
    groups, tile, lanes = own_ref.shape
    me = lax.axis_index("row")
    for g in range(groups):
        chip = lax.rem(me // 2 + g, n // 2)
        own_ref[g] = pair(
            lambda q: slab_ref[:, pl.ds(pl.multiple_of(q * lanes, lanes), lanes)],
            owned_ref[2 * chip],
            owned_ref[2 * chip + 1],
            tile,
        )


def order_kernel(line_ref, inv_ref, out_ref):
    chips, tile, lanes = line_ref.shape
    for q in range(chips):
        out_ref[:, q * lanes : (q + 1) * lanes] = pair(
            lambda p: line_ref[p], inv_ref[2 * q], inv_ref[2 * q + 1], tile
        )


def gather_kernel(n, own_ref, full_ref, buf, send_sem, recv_sem):
    planes, chips = n // 4, n // 2
    groups = buf.shape[1]
    lanes = buf.shape[3]
    me, z, y, c = place(n)
    core_peer, side_peer = me + 1 - 2 * c, me + 2 - 4 * y
    buf[me] = own_ref[...]
    greet(planes, me, z, y, c)

    def copy(s, way, peer):
        return pltpu.make_async_remote_copy(
            src_ref=buf.at[s],
            dst_ref=buf.at[s],
            send_sem=send_sem.at[way, s],
            recv_sem=recv_sem.at[s],
            device_id=to(peer),
            device_id_type=MESH,
        )

    def arrive(s):
        copy(s, 0, core_peer).wait_recv()

    up, down = z < planes - 1, z > 0

    def along(k, fn):
        for sign in (1, -1):
            zz = z + sign * k
            @pl.when((zz >= 0) & (zz < planes))
            def _():
                fn(zz, sign)
            if k == 0:
                break

    @pl.when(up)
    def _():
        copy(me, 3, me + 4).start()

    @pl.when(down)
    def _():
        copy(me, 2, me - 4).start()

    copy(me, 1, side_peer).start()
    copy(me, 0, core_peer).start()

    def from_side(zz, sign):
        s = (zz * 2 + 1 - y) * 2 + c
        arrive(s)
        copy(s, 0, core_peer).start()

    for k in range(1, planes):
        def from_plane(zz, sign):
            s = (zz * 2 + y) * 2 + c
            arrive(s)
            if k < planes - 1:
                if sign > 0:
                    @pl.when(down)
                    def _():
                        copy(s, 2, me - 4).start()
                else:
                    @pl.when(up)
                    def _():
                        copy(s, 3, me + 4).start()
            copy(s, 1, side_peer).start()
            copy(s, 0, core_peer).start()

        along(k, from_plane)
        along(k - 1, from_side)
    along(planes - 1, from_side)
    for k in range(planes):
        def from_core(zz, sign):
            for side in range(2):
                arrive((zz * 2 + side) * 2 + 1 - c)

        along(k, from_core)

    @pl.loop(0, chips)
    def _(m):
        rows = pl.ds(pl.multiple_of(m * lanes, lanes), lanes)
        for g in range(groups):
            other = lax.rem(m + g, chips)
            cols = pl.ds(pl.multiple_of(other * lanes, lanes), lanes)
            block = jnp.concatenate([buf[2 * m, g], buf[2 * m + 1, g]], axis=0)
            full_ref[rows, cols] = block
            if g and 2 * g != chips:
                full_ref[cols, rows] = block.T

    for k in range(planes):
        def sent(zz, sign):
            s = (zz * 2 + y) * 2 + c
            copy(s, 0, core_peer).wait_send()
            copy(s, 1, side_peer).wait_send()
            copy((zz * 2 + 1 - y) * 2 + c, 0, core_peer).wait_send()
            if k == 0 or (k < planes - 1 and sign < 0):
                @pl.when(up)
                def _():
                    copy(s, 3, me + 4).wait_send()
            if k == 0 or (k < planes - 1 and sign > 0):
                @pl.when(down)
                def _():
                    copy(s, 2, me - 4).wait_send()

        along(k, sent)


def compute_kernel(
    n, groups, full_ref, lists_ref, counts_ref, owned_ref, phi_ref, grad_ref, wts_ref,
    out_ref, inv_out, high, lows, acc, inv, pos, has,
):
    step = pl.program_id(0)
    slots = lists_ref.shape[1]
    funcs = phi_ref.shape[1]
    tile = funcs // slots
    lanes = 2 * tile
    chips = n // 2
    me = lax.axis_index("row")

    @pl.when(step == 0)
    def _():
        count = counts_ref[me]

        @pl.loop(0, n)
        def _(r):
            inv[owned_ref[r]] = r
            pos[r] = 0
            has[r] = 0

        @pl.loop(0, n)
        def _(r):
            inv_out[r] = inv[r]

        for k in range(slots):
            owner = inv[lists_ref[me, k]]
            pos[owner] = k
            has[owner] = (k < count).astype(jnp.int32)

        @pl.loop(0, slots)
        def _(i):
            rows = pl.ds(pl.multiple_of(inv[lists_ref[me, i]] * tile, tile), tile)
            dest = pl.ds(pl.multiple_of(i * tile, tile), tile)
            for j in range(slots // 2):
                block = pair(
                    lambda q: full_ref[rows, pl.ds(pl.multiple_of(q * lanes, lanes), lanes)],
                    inv[lists_ref[me, 2 * j]],
                    inv[lists_ref[me, 2 * j + 1]],
                    tile,
                )
                slot = 2 * j + lax.broadcasted_iota(jnp.int32, block.shape, 1) // tile
                keep = (slot < count) & (jnp.full(block.shape, i, jnp.int32) < count)
                block = jnp.where(keep, block, 0.0)
                top = block.astype(BF16)
                high[dest, j * lanes : (j + 1) * lanes] = top
                lows[dest, j * lanes : (j + 1) * lanes] = (block - top.astype(F32)).astype(BF16)

        acc[...] = jnp.zeros_like(acc)

    phi = phi_ref[...]
    phi_high = phi.astype(BF16)
    phi_low = (phi - phi_high.astype(F32)).astype(BF16)

    def dot(a, b):
        return jnp.dot(a, b, preferred_element_type=F32)

    mixed = dot(phi_high, high[...]) + dot(phi_high, lows[...]) + dot(phi_low, high[...])

    def row_sum(prod):
        part = prod[:, :lanes]
        for q in range(1, funcs // lanes):
            part = part + prod[:, q * lanes : (q + 1) * lanes]
        return jnp.sum(part.T, axis=0, keepdims=True)

    rho = row_sum(mixed * phi)
    slope = [2.0 * row_sum(mixed * grad_ref[k]) for k in range(3)]
    sigma = slope[0] * slope[0] + slope[1] * slope[1] + slope[2] * slope[2]
    root = jnp.exp(jnp.log(rho) * (1.0 / 3.0))
    four = rho * root
    reduced = sigma / (SCALE * (four * four))
    inner = 1.0 / (1.0 + (MU_COEF / KAPPA) * reduced)
    factor = 1.0 + KAPPA - KAPPA * inner
    change = MU_COEF * inner
    vrho = -COEF * root * ((4.0 / 3.0) * factor - (8.0 / 3.0) * ((reduced * inner) * change))
    vsigma = (-COEF / SCALE) * (change * inner) / four
    wts = wts_ref[...]
    rows = [0.5 * wts * vrho] + [2.0 * wts * vsigma * s for s in slope]
    scal = jnp.concatenate(rows + rows, axis=0).T
    zeta = (
        scal[:, 0:1] * phi
        + scal[:, 1:2] * grad_ref[0]
        + scal[:, 2:3] * grad_ref[1]
        + scal[:, 3:4] * grad_ref[2]
    )
    zeta_high = zeta.astype(BF16)
    zeta_low = (zeta - zeta_high.astype(F32)).astype(BF16)

    def tdot(a, b):
        return lax.dot_general(a, b, (((0,), (0,)), ((), ())), preferred_element_type=F32)

    acc[...] += tdot(phi_high, zeta_high) + tdot(phi_high, zeta_low) + tdot(phi_low, zeta_high)

    @pl.when(step == pl.num_programs(0) - 1)
    def _():
        acc[...] = acc[...] + acc[...].T

        @pl.loop(0, n)
        def _(r):
            rows = pl.ds(pl.multiple_of(pos[r] * tile, tile), tile)
            for g in range(groups):
                chip = lax.rem(r // 2 + g, chips)
                block = pair(
                    lambda q: acc[rows, pl.ds(pl.multiple_of(q * lanes, lanes), lanes)],
                    pos[2 * chip],
                    pos[2 * chip + 1],
                    tile,
                )
                low = lax.broadcasted_iota(jnp.int32, block.shape, 1) < tile
                keep = jnp.where(
                    low,
                    jnp.full(block.shape, has[r] * has[2 * chip], jnp.int32),
                    jnp.full(block.shape, has[r] * has[2 * chip + 1], jnp.int32),
                )
                out_ref[r, g] = jnp.where(keep == 1, block, 0.0)


def reduce_kernel(
    n, part_ref, line, core_in, side_in, plane_in, msg, got,
    core_sem, side_sem, plane_sem, msg_sem,
):
    planes, chips = n // 4, n // 2
    groups, tile = part_ref.shape[1], part_ref.shape[2]
    lanes = 2 * tile
    half = tile // 2
    me, z, y, c = place(n)
    core_peer, side_peer = me + 1 - 2 * c, me + 2 - 4 * y
    chip = me // 2
    mirrored = [g for g in range(1, groups) if 2 * g != chips]

    barrier = pltpu.get_barrier_semaphore()

    @pl.loop(1, n)
    def _(k):
        pl.semaphore_signal(
            barrier, inc=1, device_id=to(lax.rem(me + k, n)), device_id_type=MESH
        )

    pl.semaphore_wait(barrier, n - 1)

    def remote(src, dst, sems, slot, peer):
        return pltpu.make_async_remote_copy(
            src_ref=src, dst_ref=dst, send_sem=sems.at[0, slot], recv_sem=sems.at[1, slot],
            device_id=to(peer), device_id_type=MESH,
        )

    def by_core(zz, side):
        j = zz * 2 + side
        return remote(part_ref.at[2 * j + 1 - c], core_in.at[j], core_sem, j, core_peer)

    def by_side(zz):
        return remote(core_in.at[zz * 2 + 1 - y], side_in.at[zz], side_sem, zz, side_peer)

    def by_plane(zz, sign):
        way = 0 if sign > 0 else 1
        return remote(
            side_in.at[zz], plane_in.at[way, zz], plane_sem, way * planes + zz, me + 4 * sign
        )

    def far_to_near(fn):
        for k in range(planes - 1, -1, -1):
            for sign in (1, -1):
                zz = z + sign * k
                @pl.when((zz >= 0) & (zz < planes))
                def _():
                    fn(zz, k, sign)
                if k == 0:
                    break

    def start_core(zz, k, sign):
        by_core(zz, 1 - y).start()
        by_core(zz, y).start()

    far_to_near(start_core)

    def side_step(zz, k, sign):
        by_core(zz, 1 - y).wait_recv()
        j = zz * 2 + 1 - y
        core_in[j] = core_in[j] + part_ref[2 * j + c]
        by_side(zz).start()

    far_to_near(side_step)

    def plane_step(zz, k, sign):
        by_core(zz, y).wait_recv()
        j = zz * 2 + y
        core_in[j] = core_in[j] + part_ref[2 * j + c]
        by_side(zz).wait_recv()
        side_in[zz] = side_in[zz] + core_in[j]
        if k:
            behind = (z > 0) if sign > 0 else (z < planes - 1)

            @pl.when(behind)
            def _():
                by_plane(zz, sign).wait_recv()
                side_in[zz] = side_in[zz] + plane_in[0 if sign > 0 else 1, zz]

            by_plane(zz, sign).start()

    far_to_near(plane_step)

    for ok, sign in ((z > 0, 1), (z < planes - 1, -1)):
        @pl.when(ok)
        def _():
            by_plane(z, sign).wait_recv()
            side_in[z] = side_in[z] + plane_in[0 if sign > 0 else 1, z]

    def by_mirror(i, g, core):
        return pltpu.make_async_remote_copy(
            src_ref=msg.at[i, core],
            dst_ref=got.at[i, c],
            send_sem=msg_sem.at[0, 2 * i + core],
            recv_sem=msg_sem.at[1, 2 * i + c],
            device_id=to(lax.rem(chip + g, chips) * 2 + core),
            device_id_type=MESH,
        )

    for i, g in enumerate(mirrored):
        for core in range(2):
            block = side_in[z, g, :, core * tile : (core + 1) * tile]
            msg[i, core] = jnp.concatenate([block[:half], block[half:]], axis=1)
            by_mirror(i, g, core).start()
    for g in range(groups):
        line[lax.rem(chip + g, chips)] = side_in[z, g]
    for i, g in enumerate(mirrored):
        blocks = []
        for core in range(2):
            pltpu.make_async_remote_copy(
                src_ref=msg.at[i, core],
                dst_ref=got.at[i, core],
                send_sem=msg_sem.at[0, 2 * i + core],
                recv_sem=msg_sem.at[1, 2 * i + core],
                device_id=to(core_peer),
                device_id_type=MESH,
            ).wait_recv()
            wide = got[i, core]
            blocks.append(jnp.concatenate([wide[:, :tile], wide[:, tile:]], axis=0))
        line[lax.rem(chip + chips - g, chips)] = jnp.concatenate(blocks, axis=0).T
    def sent(zz, k, sign):
        by_core(zz, y).wait_send()
        by_core(zz, 1 - y).wait_send()
        by_side(zz).wait_send()
        if k:
            by_plane(zz, sign).wait_send()

    far_to_near(sent)
    for i, g in enumerate(mirrored):
        for core in range(2):
            by_mirror(i, g, core).wait_send()


def shards(basis_values, basis_grads, weights, tile_lists, tile_counts, owned_rows, density_slabs):
    n = lax.axis_size("row")
    tile, width = density_slabs.shape
    npts, funcs = basis_values.shape
    planes, chips = n // 4, n // 2
    groups = chips // 2 + 1
    lanes = 2 * tile
    vmem = pl.BlockSpec(memory_space=pltpu.VMEM)
    smem = pl.BlockSpec(memory_space=pltpu.SMEM)
    dma = pltpu.SemaphoreType.DMA
    own = pl.pallas_call(
        functools.partial(pack_kernel, n),
        out_shape=jax.ShapeDtypeStruct((groups, tile, lanes), F32),
        in_specs=[vmem, smem],
        out_specs=vmem,
        name="pack_density",
    )(density_slabs, owned_rows)
    full = pl.pallas_call(
        functools.partial(gather_kernel, n),
        out_shape=jax.ShapeDtypeStruct((width, width), F32),
        in_specs=[vmem],
        out_specs=vmem,
        scratch_shapes=[
            pltpu.VMEM((n, groups, tile, lanes), F32),
            dma((4, n)),
            dma((n,)),
        ],
        compiler_params=pltpu.CompilerParams(
            collective_id=0, has_side_effects=True, vmem_limit_bytes=VMEM_LIMIT
        ),
        name="gather_density",
    )(own)
    chunk = min(npts, 256)
    part, inv = pl.pallas_call(
        functools.partial(compute_kernel, n, groups),
        grid=(npts // chunk,),
        out_shape=(
            jax.ShapeDtypeStruct((n, groups, tile, lanes), F32),
            jax.ShapeDtypeStruct((n,), jnp.int32),
        ),
        in_specs=[
            vmem, smem, smem, smem,
            pl.BlockSpec((chunk, funcs), lambda i: (i, 0)),
            pl.BlockSpec((3, chunk, funcs), lambda i: (0, i, 0)),
            pl.BlockSpec((1, chunk), lambda i: (0, i)),
        ],
        out_specs=(vmem, smem),
        scratch_shapes=[
            pltpu.VMEM((funcs, funcs), BF16),
            pltpu.VMEM((funcs, funcs), BF16),
            pltpu.VMEM((funcs, funcs), F32),
            pltpu.SMEM((n,), jnp.int32),
            pltpu.SMEM((n,), jnp.int32),
            pltpu.SMEM((n,), jnp.int32),
        ],
        compiler_params=pltpu.CompilerParams(vmem_limit_bytes=VMEM_LIMIT),
        name="batch_potential",
    )(
        full, tile_lists, tile_counts, owned_rows,
        basis_values, basis_grads, weights.reshape(1, npts),
    )
    mirrored = len([g for g in range(1, groups) if 2 * g != chips])
    line = pl.pallas_call(
        functools.partial(reduce_kernel, n),
        out_shape=jax.ShapeDtypeStruct((chips, tile, lanes), F32),
        in_specs=[vmem],
        out_specs=vmem,
        scratch_shapes=[
            pltpu.VMEM((chips, groups, tile, lanes), F32),
            pltpu.VMEM((planes, groups, tile, lanes), F32),
            pltpu.VMEM((2, planes, groups, tile, lanes), F32),
            pltpu.VMEM((mirrored, 2, tile // 2, lanes), F32),
            pltpu.VMEM((mirrored, 2, tile // 2, lanes), F32),
            dma((2, chips)),
            dma((2, planes)),
            dma((2, 2 * planes)),
            dma((2, 2 * mirrored)),
        ],
        compiler_params=pltpu.CompilerParams(
            collective_id=1, has_side_effects=True, vmem_limit_bytes=VMEM_LIMIT
        ),
        name="reduce_potential",
    )(part)
    return pl.pallas_call(
        order_kernel,
        out_shape=jax.ShapeDtypeStruct((tile, width), F32),
        in_specs=[vmem, smem],
        out_specs=vmem,
        name="order_columns",
    )(line, inv)


def solution(mesh):
    in_specs = (
        P(("parts", "row"), None),
        P(None, ("parts", "row"), None),
        P(("parts", "row")),
        P("parts", None),
        P("parts"),
        P("parts"),
        P(("parts", "row"), None),
    )
    out_specs = P(("parts", "row"), None)
    return jax.shard_map(shards, mesh=mesh, in_specs=in_specs, out_specs=out_specs, check_vma=False)
```

```python
import functools
import math

import jax
import jax.numpy as jnp
from jax import lax
from jax.experimental import pallas as pl
from jax.experimental.pallas import tpu as pltpu
from jax.sharding import PartitionSpec as P

KAPPA = 0.804
MU_COEF = 0.2195
COEF = 0.75 * (3.0 / math.pi) ** (1.0 / 3.0)
SCALE = 4.0 * (3.0 * math.pi**2) ** (2.0 / 3.0)
MESH = pl.DeviceIdType.MESH
PIECES = 2
VMEM_LIMIT = 60 * 1024 * 1024
F32, BF16 = jnp.float32, jnp.bfloat16


def pair(load, first, second, tile):
    left, right = load(lax.div(first, 2)), load(lax.div(second, 2))
    low = lax.broadcasted_iota(jnp.int32, left.shape, 1) < tile
    odd = jnp.full(left.shape, lax.rem(first, 2), jnp.int32) == 1
    even = jnp.full(left.shape, lax.rem(second, 2), jnp.int32) == 0
    left = jnp.where(odd, pltpu.roll(left, tile, 1), left)
    right = jnp.where(even, pltpu.roll(right, tile, 1), right)
    return jnp.where(low, left, right)


def cut(groups):
    return [groups * h // PIECES for h in range(PIECES + 1)]


def chosen(columns, first, second, tile):
    shape = columns[0].shape
    low = lax.broadcasted_iota(jnp.int32, shape, 1) < tile
    want = jnp.where(low, jnp.full(shape, first, jnp.int32), jnp.full(shape, second, jnp.int32))
    straight = jnp.where(low, 0, 1)
    same = jnp.zeros(shape, F32)
    swap = jnp.zeros(shape, F32)
    back = pltpu.roll(want, tile, 1)
    for q, column in enumerate(columns):
        same = jnp.where(want == 2 * q + straight, column, same)
        swap = jnp.where(back == 2 * q + straight, column, swap)
    turned = pltpu.roll(swap, tile, 1)
    return jnp.where(want % 2 == straight, same, turned)


def place(n):
    me = lax.axis_index("row")
    return me, me // 4, (me // 2) % 2, me % 2


def to(row):
    return {"row": row}


def greet(planes, me, z, y, c):
    barrier = pltpu.get_barrier_semaphore()
    for ok, peer in neighbours(planes, me, z, y, c):
        @pl.when(ok)
        def _():
            pl.semaphore_signal(barrier, inc=1, device_id=to(peer), device_id_type=MESH)
    peers = 2 + (z > 0).astype(jnp.int32) + (z < planes - 1).astype(jnp.int32)
    pl.semaphore_wait(barrier, peers)


def neighbours(planes, me, z, y, c):
    return (
        (z >= 0, me + 1 - 2 * c),
        (z >= 0, me + 2 - 4 * y),
        (z > 0, me - 4),
        (z < planes - 1, me + 4),
    )


def gather_kernel(n, slab_ref, owned_ref, full_ref, buf, send_sem, recv_sem):
    planes, chips = n // 4, n // 2
    groups = buf.shape[1]
    lanes = buf.shape[3]
    cuts = cut(groups)
    halves = range(len(cuts) - 1)
    me, z, y, c = place(n)
    core_peer, side_peer = me + 1 - 2 * c, me + 2 - 4 * y
    columns = [slab_ref[:, q * lanes : (q + 1) * lanes] for q in range(chips)]
    for g in range(groups):
        chip = lax.rem(me // 2 + g, chips)
        buf[me, g] = chosen(columns, owned_ref[2 * chip], owned_ref[2 * chip + 1], lanes // 2)
    greet(planes, me, z, y, c)

    def copy(s, way, peer, h):
        part = buf.at[s, pl.ds(cuts[h], cuts[h + 1] - cuts[h])]
        return pltpu.make_async_remote_copy(
            src_ref=part,
            dst_ref=part,
            send_sem=send_sem.at[h, way, s],
            recv_sem=recv_sem.at[h, s],
            device_id=to(peer),
            device_id_type=MESH,
        )

    def arrive(s, h):
        copy(s, 0, core_peer, h).wait_recv()

    up, down = z < planes - 1, z > 0

    def along(k, fn):
        for sign in (1, -1):
            zz = z + sign * k
            @pl.when((zz >= 0) & (zz < planes))
            def _():
                fn(zz, sign)
            if k == 0:
                break

    for h in halves:
        @pl.when(up)
        def _():
            copy(me, 3, me + 4, h).start()

        @pl.when(down)
        def _():
            copy(me, 2, me - 4, h).start()

        copy(me, 1, side_peer, h).start()
        copy(me, 0, core_peer, h).start()

    def ends(zz):
        return (zz == 0) | (zz == planes - 1)

    def crossed(zz, sign, k, h, act):
        s = (zz * 2 + 1 - y) * 2 + c
        if h == len(cuts) - 2:
            if k == 0 or sign < 0:
                @pl.when(ends(zz) & up)
                def _():
                    act(copy(s, 3, me + 4, h))
            if k == 0 or sign > 0:
                @pl.when(ends(zz) & down)
                def _():
                    act(copy(s, 2, me - 4, h))

    def over(zz, k, h, act):
        s = (zz * 2 + y) * 2 + c
        if k and h == len(cuts) - 2:
            @pl.when(jnp.logical_not(ends(zz)))
            def _():
                act(copy(s, 1, side_peer, h))
        else:
            act(copy(s, 1, side_peer, h))

    def from_side(k, h):
        def fn(zz, sign):
            s = (zz * 2 + 1 - y) * 2 + c
            arrive(s, h)
            crossed(zz, sign, k, h, lambda copied: copied.start())
            copy(s, 0, core_peer, h).start()

        return fn

    def from_plane(k, h):
        def fn(zz, sign):
            s = (zz * 2 + y) * 2 + c
            arrive(s, h)
            if k < planes - 1:
                if sign > 0:
                    @pl.when(down)
                    def _():
                        copy(s, 2, me - 4, h).start()
                else:
                    @pl.when(up)
                    def _():
                        copy(s, 3, me + 4, h).start()
            over(zz, k, h, lambda copied: copied.start())
            copy(s, 0, core_peer, h).start()

        return fn

    for k in range(1, planes):
        for h in halves:
            along(k, from_plane(k, h))
            along(k - 1, from_side(k - 1, h))
    for h in halves:
        along(planes - 1, from_side(planes - 1, h))
    for k in range(planes):
        def from_core(zz, sign):
            for side in range(2):
                for h in halves:
                    arrive((zz * 2 + side) * 2 + 1 - c, h)

        along(k, from_core)

    @pl.loop(0, chips)
    def _(m):
        rows = pl.ds(pl.multiple_of(m * lanes, lanes), lanes)
        for g in range(groups):
            other = lax.rem(m + g, chips)
            cols = pl.ds(pl.multiple_of(other * lanes, lanes), lanes)
            block = jnp.concatenate([buf[2 * m, g], buf[2 * m + 1, g]], axis=0)
            full_ref[rows, cols] = block
            if g and 2 * g != chips:
                full_ref[cols, rows] = block.T

    for k in range(planes):
        for h in halves:
            def sent(zz, sign):
                s = (zz * 2 + y) * 2 + c
                copy(s, 0, core_peer, h).wait_send()
                over(zz, k, h, lambda copied: copied.wait_send())
                crossed(zz, sign, k, h, lambda copied: copied.wait_send())
                copy((zz * 2 + 1 - y) * 2 + c, 0, core_peer, h).wait_send()
                if k == 0 or (k < planes - 1 and sign < 0):
                    @pl.when(up)
                    def _():
                        copy(s, 3, me + 4, h).wait_send()
                if k == 0 or (k < planes - 1 and sign > 0):
                    @pl.when(down)
                    def _():
                        copy(s, 2, me - 4, h).wait_send()

            along(k, sent)


def compute_kernel(
    n, groups, full_ref, lists_ref, counts_ref, owned_ref, phi_ref, grad_ref, wts_ref,
    out_ref, inv_out, high, lows, acc, turned, inv, pos, has,
):
    step = pl.program_id(0)
    slots = lists_ref.shape[0]
    funcs = phi_ref.shape[1]
    tile = funcs // slots
    lanes = 2 * tile
    chips = n // 2
    me = lax.axis_index("row")

    @pl.when(step == 0)
    def _():
        count = counts_ref[me]

        @pl.loop(0, n)
        def _(r):
            inv[owned_ref[r]] = r
            pos[r] = 0
            has[r] = 0

        @pl.loop(0, n)
        def _(r):
            inv_out[r] = inv[r]

        for k in range(slots):
            owner = inv[lists_ref[k, me]]
            pos[owner] = k
            has[owner] = (k < count).astype(jnp.int32)

        @pl.loop(0, slots)
        def _(i):
            rows = pl.ds(pl.multiple_of(inv[lists_ref[i, me]] * tile, tile), tile)
            dest = pl.ds(pl.multiple_of(i * tile, tile), tile)
            for j in range(slots // 2):
                block = pair(
                    lambda q: full_ref[rows, pl.ds(pl.multiple_of(q * lanes, lanes), lanes)],
                    inv[lists_ref[2 * j, me]],
                    inv[lists_ref[2 * j + 1, me]],
                    tile,
                )
                slot = 2 * j + lax.broadcasted_iota(jnp.int32, block.shape, 1) // tile
                keep = (slot < count) & (jnp.full(block.shape, i, jnp.int32) < count)
                block = jnp.where(keep, block, 0.0)
                top = block.astype(BF16)
                high[dest, j * lanes : (j + 1) * lanes] = top
                lows[dest, j * lanes : (j + 1) * lanes] = (block - top.astype(F32)).astype(BF16)

        acc[...] = jnp.zeros_like(acc)

    phi = phi_ref[...]
    phi_high = phi.astype(BF16)
    phi_low = (phi - phi_high.astype(F32)).astype(BF16)

    def dot(a, b):
        return jnp.dot(a, b, preferred_element_type=F32)

    mixed = dot(phi_high, high[...]) + dot(phi_high, lows[...]) + dot(phi_low, high[...])

    def row_sum(prod):
        part = prod[:, :lanes]
        for q in range(1, funcs // lanes):
            part = part + prod[:, q * lanes : (q + 1) * lanes]
        return jnp.sum(part.T, axis=0, keepdims=True)

    rho = row_sum(mixed * phi)
    slope = [2.0 * row_sum(mixed * grad_ref[k]) for k in range(3)]
    sigma = slope[0] * slope[0] + slope[1] * slope[1] + slope[2] * slope[2]
    root = jnp.exp(jnp.log(rho) * (1.0 / 3.0))
    four = rho * root
    reduced = sigma / (SCALE * (four * four))
    inner = 1.0 / (1.0 + (MU_COEF / KAPPA) * reduced)
    factor = 1.0 + KAPPA - KAPPA * inner
    change = MU_COEF * inner
    vrho = -COEF * root * ((4.0 / 3.0) * factor - (8.0 / 3.0) * ((reduced * inner) * change))
    vsigma = (-COEF / SCALE) * (change * inner) / four
    wts = wts_ref[...]
    rows = [0.5 * wts * vrho] + [2.0 * wts * vsigma * s for s in slope]
    scal = jnp.concatenate(rows + rows, axis=0).T
    zeta = (
        scal[:, 0:1] * phi
        + scal[:, 1:2] * grad_ref[0]
        + scal[:, 2:3] * grad_ref[1]
        + scal[:, 3:4] * grad_ref[2]
    )
    zeta_high = zeta.astype(BF16)
    zeta_low = (zeta - zeta_high.astype(F32)).astype(BF16)

    def tdot(a, b):
        return lax.dot_general(a, b, (((0,), (0,)), ((), ())), preferred_element_type=F32)

    acc[...] += tdot(phi_high, zeta_high) + tdot(phi_high, zeta_low) + tdot(phi_low, zeta_high)

    @pl.when(step == pl.num_programs(0) - 1)
    def _():
        both = acc[...] + acc[...].T
        for q in range(funcs // lanes):
            block = both[:, q * lanes : (q + 1) * lanes]
            turned[2 * q] = block
            turned[2 * q + 1] = pltpu.roll(block, tile, 1)
        low = lax.broadcasted_iota(jnp.int32, (tile, lanes), 1) < tile

        @pl.loop(0, chips)
        def _(chip):
            first, second = pos[2 * chip], pos[2 * chip + 1]
            other = 2 * lax.div(second, 2) + 1 - lax.rem(second, 2)
            keep = jnp.where(low, has[2 * chip].astype(F32), has[2 * chip + 1].astype(F32))
            for g in range(groups):
                for core in range(2):
                    r = 2 * lax.rem(chip + chips - g, chips) + core
                    rows = pl.ds(pl.multiple_of(pos[r] * tile, tile), tile)
                    block = jnp.where(low, turned[first, rows], turned[other, rows])
                    out_ref[r, g] = block * (keep * has[r].astype(F32))


def reduce_kernel(
    n, part_ref, inv_ref, out_ref, line, core_in, side_in, plane_in, msg, got,
    core_sem, side_sem, plane_sem, msg_sem,
):
    planes, chips = n // 4, n // 2
    groups, tile = part_ref.shape[1], part_ref.shape[2]
    lanes = 2 * tile
    half = tile // 2
    me, z, y, c = place(n)
    core_peer, side_peer = me + 1 - 2 * c, me + 2 - 4 * y
    chip = me // 2
    mirrored = [g for g in range(1, groups) if 2 * g != chips]

    barrier = pltpu.get_barrier_semaphore()

    @pl.loop(1, n)
    def _(k):
        pl.semaphore_signal(
            barrier, inc=1, device_id=to(lax.rem(me + k, n)), device_id_type=MESH
        )

    pl.semaphore_wait(barrier, n - 1)

    cuts = cut(groups)
    halves = range(len(cuts) - 1)

    def group(h):
        return pl.ds(cuts[h], cuts[h + 1] - cuts[h])

    def remote(src, dst, sems, h, slot, peer):
        return pltpu.make_async_remote_copy(
            src_ref=src, dst_ref=dst,
            send_sem=sems.at[0, h, slot], recv_sem=sems.at[1, h, slot],
            device_id=to(peer), device_id_type=MESH,
        )

    def by_core(zz, side, h):
        j = zz * 2 + side
        return remote(
            part_ref.at[2 * j + 1 - c, group(h)], core_in.at[j, group(h)], core_sem, h, j, core_peer
        )

    def by_side(zz, h):
        return remote(
            core_in.at[zz * 2 + 1 - y, group(h)], side_in.at[zz, group(h)],
            side_sem, h, zz, side_peer,
        )

    def by_plane(zz, sign, h):
        way = 0 if sign > 0 else 1
        return remote(
            side_in.at[zz, group(h)], plane_in.at[way, zz, group(h)],
            plane_sem, h, way * planes + zz, me + 4 * sign,
        )

    def far_to_near(fn):
        for k in range(planes - 1, -1, -1):
            for h in halves:
                for sign in (1, -1):
                    zz = z + sign * k
                    @pl.when((zz >= 0) & (zz < planes))
                    def _():
                        fn(zz, k, sign, h)
                    if k == 0:
                        break

    def start_core(zz, k, sign, h):
        by_core(zz, 1 - y, h).start()
        by_core(zz, y, h).start()

    far_to_near(start_core)

    def side_step(zz, k, sign, h):
        by_core(zz, 1 - y, h).wait_recv()
        j = zz * 2 + 1 - y
        core_in[j, group(h)] = core_in[j, group(h)] + part_ref[2 * j + c, group(h)]
        by_side(zz, h).start()

    far_to_near(side_step)

    def plane_step(zz, k, sign, h):
        by_core(zz, y, h).wait_recv()
        j = zz * 2 + y
        by_side(zz, h).wait_recv()
        total = side_in[zz, group(h)] + (core_in[j, group(h)] + part_ref[2 * j + c, group(h)])
        side_in[zz, group(h)] = total
        if k:
            behind = (z > 0) if sign > 0 else (z < planes - 1)

            @pl.when(behind)
            def _():
                by_plane(zz, sign, h).wait_recv()
                way = 0 if sign > 0 else 1
                side_in[zz, group(h)] = side_in[zz, group(h)] + plane_in[way, zz, group(h)]

            by_plane(zz, sign, h).start()

    far_to_near(plane_step)

    for h in halves:
        for ok, sign in ((z > 0, 1), (z < planes - 1, -1)):
            @pl.when(ok)
            def _():
                by_plane(z, sign, h).wait_recv()
                way = 0 if sign > 0 else 1
                side_in[z, group(h)] = side_in[z, group(h)] + plane_in[way, z, group(h)]

    def by_mirror(i, g, core):
        return pltpu.make_async_remote_copy(
            src_ref=msg.at[i, core],
            dst_ref=got.at[i, c],
            send_sem=msg_sem.at[0, 2 * i + core],
            recv_sem=msg_sem.at[1, 2 * i + c],
            device_id=to(lax.rem(chip + g, chips) * 2 + core),
            device_id_type=MESH,
        )

    for i, g in enumerate(mirrored):
        for core in range(2):
            block = side_in[z, g, :, core * tile : (core + 1) * tile]
            msg[i, core] = jnp.concatenate([block[:half], block[half:]], axis=1)
            by_mirror(i, g, core).start()
    for g in range(groups):
        line[lax.rem(chip + g, chips)] = side_in[z, g]
    for i, g in enumerate(mirrored):
        blocks = []
        for core in range(2):
            pltpu.make_async_remote_copy(
                src_ref=msg.at[i, core],
                dst_ref=got.at[i, core],
                send_sem=msg_sem.at[0, 2 * i + core],
                recv_sem=msg_sem.at[1, 2 * i + core],
                device_id=to(core_peer),
                device_id_type=MESH,
            ).wait_recv()
            wide = got[i, core]
            blocks.append(jnp.concatenate([wide[:, :tile], wide[:, tile:]], axis=0))
        line[lax.rem(chip + chips - g, chips)] = jnp.concatenate(blocks, axis=0).T
    columns = [line[q] for q in range(chips)]
    for q in range(chips):
        out_ref[:, q * lanes : (q + 1) * lanes] = chosen(
            columns, inv_ref[2 * q], inv_ref[2 * q + 1], tile
        )

    def sent(zz, k, sign, h):
        by_core(zz, y, h).wait_send()
        by_core(zz, 1 - y, h).wait_send()
        by_side(zz, h).wait_send()
        if k:
            by_plane(zz, sign, h).wait_send()

    far_to_near(sent)
    for i, g in enumerate(mirrored):
        for core in range(2):
            by_mirror(i, g, core).wait_send()


def shards(basis_values, basis_grads, weights, tile_lists, tile_counts, owned_rows, density_slabs):
    n = lax.axis_size("row")
    tile, width = density_slabs.shape
    npts, funcs = basis_values.shape
    planes, chips = n // 4, n // 2
    groups = chips // 2 + 1
    lanes = 2 * tile
    vmem = pl.BlockSpec(memory_space=pltpu.VMEM)
    smem = pl.BlockSpec(memory_space=pltpu.SMEM)
    dma = pltpu.SemaphoreType.DMA
    full = pl.pallas_call(
        functools.partial(gather_kernel, n),
        out_shape=jax.ShapeDtypeStruct((width, width), F32),
        in_specs=[vmem, smem],
        out_specs=vmem,
        scratch_shapes=[
            pltpu.VMEM((n, groups, tile, lanes), F32),
            dma((PIECES, 4, n)),
            dma((PIECES, n)),
        ],
        compiler_params=pltpu.CompilerParams(
            collective_id=0, has_side_effects=True, vmem_limit_bytes=VMEM_LIMIT
        ),
        name="gather_density",
    )(density_slabs, owned_rows)
    chunk = min(npts, 2**18 // funcs)
    part, inv = pl.pallas_call(
        functools.partial(compute_kernel, n, groups),
        grid=(npts // chunk,),
        out_shape=(
            jax.ShapeDtypeStruct((n, groups, tile, lanes), F32),
            jax.ShapeDtypeStruct((n,), jnp.int32),
        ),
        in_specs=[
            vmem, smem, smem, smem,
            pl.BlockSpec((chunk, funcs), lambda i: (i, 0)),
            pl.BlockSpec((3, chunk, funcs), lambda i: (0, i, 0)),
            pl.BlockSpec((1, chunk), lambda i: (0, i)),
        ],
        out_specs=(vmem, smem),
        scratch_shapes=[
            pltpu.VMEM((funcs, funcs), BF16),
            pltpu.VMEM((funcs, funcs), BF16),
            pltpu.VMEM((funcs, funcs), F32),
            pltpu.VMEM((funcs // tile, funcs, lanes), F32),
            pltpu.SMEM((n,), jnp.int32),
            pltpu.SMEM((n,), jnp.int32),
            pltpu.SMEM((n,), jnp.int32),
        ],
        compiler_params=pltpu.CompilerParams(vmem_limit_bytes=VMEM_LIMIT),
        name="batch_potential",
    )(
        full, tile_lists.T, tile_counts, owned_rows,
        basis_values, basis_grads, weights.reshape(1, npts),
    )
    mirrored = len([g for g in range(1, groups) if 2 * g != chips])
    return pl.pallas_call(
        functools.partial(reduce_kernel, n),
        out_shape=jax.ShapeDtypeStruct((tile, width), F32),
        in_specs=[vmem, smem],
        out_specs=vmem,
        scratch_shapes=[
            pltpu.VMEM((chips, tile, lanes), F32),
            pltpu.VMEM((chips, groups, tile, lanes), F32),
            pltpu.VMEM((planes, groups, tile, lanes), F32),
            pltpu.VMEM((2, planes, groups, tile, lanes), F32),
            pltpu.VMEM((mirrored, 2, tile // 2, lanes), F32),
            pltpu.VMEM((mirrored, 2, tile // 2, lanes), F32),
            dma((2, PIECES, chips)),
            dma((2, PIECES, planes)),
            dma((2, PIECES, 2 * planes)),
            dma((2, 2 * mirrored)),
        ],
        compiler_params=pltpu.CompilerParams(
            collective_id=1, has_side_effects=True, vmem_limit_bytes=VMEM_LIMIT
        ),
        name="reduce_potential",
    )(part, inv)


def solution(mesh):
    in_specs = (
        P(("parts", "row"), None),
        P(None, ("parts", "row"), None),
        P(("parts", "row")),
        P("parts", None),
        P("parts"),
        P("parts"),
        P(("parts", "row"), None),
    )
    out_specs = P(("parts", "row"), None)
    return jax.shard_map(shards, mesh=mesh, in_specs=in_specs, out_specs=out_specs, check_vma=False)
```

```python
import functools
import math

import jax
import jax.numpy as jnp
from jax import lax
from jax.experimental import pallas as pl
from jax.experimental.pallas import tpu as pltpu
from jax.sharding import PartitionSpec as P

KAPPA = 0.804
MU_COEF = 0.2195
COEF = 0.75 * (3.0 / math.pi) ** (1.0 / 3.0)
SCALE = 4.0 * (3.0 * math.pi**2) ** (2.0 / 3.0)
MESH = pl.DeviceIdType.MESH
PIECES = 2
VMEM_LIMIT = 60 * 1024 * 1024
F32, BF16 = jnp.float32, jnp.bfloat16


def pair(load, first, second, tile):
    left, right = load(lax.div(first, 2)), load(lax.div(second, 2))
    low = lax.broadcasted_iota(jnp.int32, left.shape, 1) < tile
    odd = jnp.full(left.shape, lax.rem(first, 2), jnp.int32) == 1
    even = jnp.full(left.shape, lax.rem(second, 2), jnp.int32) == 0
    left = jnp.where(odd, pltpu.roll(left, tile, 1), left)
    right = jnp.where(even, pltpu.roll(right, tile, 1), right)
    return jnp.where(low, left, right)


def cut(groups):
    return [groups * h // PIECES for h in range(PIECES + 1)]


def chosen(columns, first, second, tile):
    shape = columns[0].shape
    low = lax.broadcasted_iota(jnp.int32, shape, 1) < tile
    want = jnp.where(low, jnp.full(shape, first, jnp.int32), jnp.full(shape, second, jnp.int32))
    straight = jnp.where(low, 0, 1)
    same = jnp.zeros(shape, F32)
    swap = jnp.zeros(shape, F32)
    back = pltpu.roll(want, tile, 1)
    for q, column in enumerate(columns):
        same = jnp.where(want == 2 * q + straight, column, same)
        swap = jnp.where(back == 2 * q + straight, column, swap)
    turned = pltpu.roll(swap, tile, 1)
    return jnp.where(want % 2 == straight, same, turned)


def place(n):
    me = lax.axis_index("row")
    return me, me // 4, (me // 2) % 2, me % 2


def to(row):
    return {"row": row}


def greet(planes, me, z, y, c):
    barrier = pltpu.get_barrier_semaphore()
    for ok, peer in neighbours(planes, me, z, y, c):
        @pl.when(ok)
        def _():
            pl.semaphore_signal(barrier, inc=1, device_id=to(peer), device_id_type=MESH)
    peers = 2 + (z > 0).astype(jnp.int32) + (z < planes - 1).astype(jnp.int32)
    pl.semaphore_wait(barrier, peers)


def neighbours(planes, me, z, y, c):
    return (
        (z >= 0, me + 1 - 2 * c),
        (z >= 0, me + 2 - 4 * y),
        (z > 0, me - 4),
        (z < planes - 1, me + 4),
    )


def gather_kernel(n, slab_ref, owned_ref, full_ref, buf, send_sem, recv_sem):
    planes, chips = n // 4, n // 2
    groups = buf.shape[1]
    lanes = buf.shape[3]
    cuts = cut(groups)
    halves = range(len(cuts) - 1)
    me, z, y, c = place(n)
    core_peer, side_peer = me + 1 - 2 * c, me + 2 - 4 * y
    columns = [slab_ref[:, q * lanes : (q + 1) * lanes] for q in range(chips)]
    for g in range(groups):
        chip = lax.rem(me // 2 + g, chips)
        buf[me, g] = chosen(columns, owned_ref[2 * chip], owned_ref[2 * chip + 1], lanes // 2)
    greet(planes, me, z, y, c)

    def copy(s, way, peer, h):
        part = buf.at[s, pl.ds(cuts[h], cuts[h + 1] - cuts[h])]
        return pltpu.make_async_remote_copy(
            src_ref=part,
            dst_ref=part,
            send_sem=send_sem.at[h, way, s],
            recv_sem=recv_sem.at[h, s],
            device_id=to(peer),
            device_id_type=MESH,
        )

    def arrive(s, h):
        copy(s, 0, core_peer, h).wait_recv()

    up, down = z < planes - 1, z > 0

    def along(k, fn):
        for sign in (1, -1):
            zz = z + sign * k
            @pl.when((zz >= 0) & (zz < planes))
            def _():
                fn(zz, sign)
            if k == 0:
                break

    for h in halves:
        @pl.when(up)
        def _():
            copy(me, 3, me + 4, h).start()

        @pl.when(down)
        def _():
            copy(me, 2, me - 4, h).start()

        copy(me, 1, side_peer, h).start()
        copy(me, 0, core_peer, h).start()

    def ends(zz):
        return (zz == 0) | (zz == planes - 1)

    def crossed(zz, sign, k, h, act):
        s = (zz * 2 + 1 - y) * 2 + c
        if h == len(cuts) - 2:
            if k == 0 or sign < 0:
                @pl.when(ends(zz) & up)
                def _():
                    act(copy(s, 3, me + 4, h))
            if k == 0 or sign > 0:
                @pl.when(ends(zz) & down)
                def _():
                    act(copy(s, 2, me - 4, h))

    def over(zz, k, h, act):
        s = (zz * 2 + y) * 2 + c
        if k and h == len(cuts) - 2:
            @pl.when(jnp.logical_not(ends(zz)))
            def _():
                act(copy(s, 1, side_peer, h))
        else:
            act(copy(s, 1, side_peer, h))

    def from_side(k, h):
        def fn(zz, sign):
            s = (zz * 2 + 1 - y) * 2 + c
            arrive(s, h)
            crossed(zz, sign, k, h, lambda copied: copied.start())
            copy(s, 0, core_peer, h).start()

        return fn

    def from_plane(k, h):
        def fn(zz, sign):
            s = (zz * 2 + y) * 2 + c
            arrive(s, h)
            if k < planes - 1:
                if sign > 0:
                    @pl.when(down)
                    def _():
                        copy(s, 2, me - 4, h).start()
                else:
                    @pl.when(up)
                    def _():
                        copy(s, 3, me + 4, h).start()
            over(zz, k, h, lambda copied: copied.start())
            copy(s, 0, core_peer, h).start()

        return fn

    for k in range(1, planes):
        for h in halves:
            along(k, from_plane(k, h))
            along(k - 1, from_side(k - 1, h))
    for h in halves:
        along(planes - 1, from_side(planes - 1, h))
    for k in range(planes):
        def from_core(zz, sign):
            for side in range(2):
                for h in halves:
                    arrive((zz * 2 + side) * 2 + 1 - c, h)

        along(k, from_core)

    @pl.loop(0, chips)
    def _(m):
        rows = pl.ds(pl.multiple_of(m * lanes, lanes), lanes)
        for g in range(groups):
            other = lax.rem(m + g, chips)
            cols = pl.ds(pl.multiple_of(other * lanes, lanes), lanes)
            block = jnp.concatenate([buf[2 * m, g], buf[2 * m + 1, g]], axis=0)
            full_ref[rows, cols] = block
            if g and 2 * g != chips:
                full_ref[cols, rows] = block.T

    for k in range(planes):
        for h in halves:
            def sent(zz, sign):
                s = (zz * 2 + y) * 2 + c
                copy(s, 0, core_peer, h).wait_send()
                over(zz, k, h, lambda copied: copied.wait_send())
                crossed(zz, sign, k, h, lambda copied: copied.wait_send())
                copy((zz * 2 + 1 - y) * 2 + c, 0, core_peer, h).wait_send()
                if k == 0 or (k < planes - 1 and sign < 0):
                    @pl.when(up)
                    def _():
                        copy(s, 3, me + 4, h).wait_send()
                if k == 0 or (k < planes - 1 and sign > 0):
                    @pl.when(down)
                    def _():
                        copy(s, 2, me - 4, h).wait_send()

            along(k, sent)


def compute_kernel(
    n, groups, full_ref, lists_ref, counts_ref, owned_ref, phi_ref, grad_ref, wts_ref,
    out_ref, inv_out, high, lows, acc, turned, inv, pos, has,
):
    step = pl.program_id(0)
    slots = lists_ref.shape[0]
    funcs = phi_ref.shape[1]
    tile = funcs // slots
    lanes = 2 * tile
    chips = n // 2
    me = lax.axis_index("row")

    @pl.when(step == 0)
    def _():
        count = counts_ref[me]

        @pl.loop(0, n)
        def _(r):
            inv[owned_ref[r]] = r
            pos[r] = 0
            has[r] = 0

        @pl.loop(0, n)
        def _(r):
            inv_out[r] = inv[r]

        for k in range(slots):
            owner = inv[lists_ref[k, me]]
            pos[owner] = k
            has[owner] = (k < count).astype(jnp.int32)

        @pl.loop(0, slots)
        def _(i):
            rows = pl.ds(pl.multiple_of(inv[lists_ref[i, me]] * tile, tile), tile)
            dest = pl.ds(pl.multiple_of(i * tile, tile), tile)
            for j in range(slots // 2):
                block = pair(
                    lambda q: full_ref[rows, pl.ds(pl.multiple_of(q * lanes, lanes), lanes)],
                    inv[lists_ref[2 * j, me]],
                    inv[lists_ref[2 * j + 1, me]],
                    tile,
                )
                slot = 2 * j + lax.broadcasted_iota(jnp.int32, block.shape, 1) // tile
                keep = (slot < count) & (jnp.full(block.shape, i, jnp.int32) < count)
                block = jnp.where(keep, block, 0.0)
                top = block.astype(BF16)
                high[dest, j * lanes : (j + 1) * lanes] = top
                lows[dest, j * lanes : (j + 1) * lanes] = (block - top.astype(F32)).astype(BF16)

        acc[...] = jnp.zeros_like(acc)

    phi = phi_ref[...]
    phi_high = phi.astype(BF16)
    phi_low = (phi - phi_high.astype(F32)).astype(BF16)

    def dot(a, b):
        return jnp.dot(a, b, preferred_element_type=F32)

    mixed = dot(phi_high, high[...]) + dot(phi_high, lows[...]) + dot(phi_low, high[...])

    def row_sum(prod):
        part = prod[:, :lanes]
        for q in range(1, funcs // lanes):
            part = part + prod[:, q * lanes : (q + 1) * lanes]
        return jnp.sum(part.T, axis=0, keepdims=True)

    rho = row_sum(mixed * phi)
    slope = [2.0 * row_sum(mixed * grad_ref[k]) for k in range(3)]
    sigma = slope[0] * slope[0] + slope[1] * slope[1] + slope[2] * slope[2]
    root = jnp.exp(jnp.log(rho) * (1.0 / 3.0))
    four = rho * root
    reduced = sigma / (SCALE * (four * four))
    inner = 1.0 / (1.0 + (MU_COEF / KAPPA) * reduced)
    factor = 1.0 + KAPPA - KAPPA * inner
    change = MU_COEF * inner
    vrho = -COEF * root * ((4.0 / 3.0) * factor - (8.0 / 3.0) * ((reduced * inner) * change))
    vsigma = (-COEF / SCALE) * (change * inner) / four
    wts = wts_ref[...]
    rows = [0.5 * wts * vrho] + [2.0 * wts * vsigma * s for s in slope]
    scal = jnp.concatenate(rows + rows, axis=0).T
    zeta = (
        scal[:, 0:1] * phi
        + scal[:, 1:2] * grad_ref[0]
        + scal[:, 2:3] * grad_ref[1]
        + scal[:, 3:4] * grad_ref[2]
    )
    zeta_high = zeta.astype(BF16)
    zeta_low = (zeta - zeta_high.astype(F32)).astype(BF16)

    def tdot(a, b):
        return lax.dot_general(a, b, (((0,), (0,)), ((), ())), preferred_element_type=F32)

    acc[...] += tdot(phi_high, zeta_high) + tdot(phi_high, zeta_low) + tdot(phi_low, zeta_high)

    @pl.when(step == pl.num_programs(0) - 1)
    def _():
        both = acc[...] + acc[...].T
        for q in range(funcs // lanes):
            block = both[:, q * lanes : (q + 1) * lanes]
            turned[2 * q] = block
            turned[2 * q + 1] = pltpu.roll(block, tile, 1)
        low = lax.broadcasted_iota(jnp.int32, (tile, lanes), 1) < tile

        @pl.loop(0, chips)
        def _(chip):
            first, second = pos[2 * chip], pos[2 * chip + 1]
            other = 2 * lax.div(second, 2) + 1 - lax.rem(second, 2)
            keep = jnp.where(low, has[2 * chip].astype(F32), has[2 * chip + 1].astype(F32))
            for g in range(groups):
                for core in range(2):
                    r = 2 * lax.rem(chip + chips - g, chips) + core
                    rows = pl.ds(pl.multiple_of(pos[r] * tile, tile), tile)
                    block = jnp.where(low, turned[first, rows], turned[other, rows])
                    out_ref[r, g] = block * (keep * has[r].astype(F32))


def reduce_kernel(
    n, part_ref, inv_ref, out_ref, line, core_in, side_in, plane_in, msg, got, held,
    core_sem, side_sem, plane_sem, msg_sem, held_sem,
):
    planes, chips = n // 4, n // 2
    groups, tile = held.shape[1], held.shape[2]
    lanes = 2 * tile
    half = tile // 2
    me, z, y, c = place(n)
    core_peer, side_peer = me + 1 - 2 * c, me + 2 - 4 * y
    chip = me // 2
    mirrored = [g for g in range(1, groups) if 2 * g != chips]

    def fetch(j):
        return pltpu.make_async_copy(part_ref.at[2 * j + c], held.at[j], held_sem.at[j])

    barrier = pltpu.get_barrier_semaphore()

    @pl.loop(1, n)
    def _(k):
        pl.semaphore_signal(
            barrier, inc=1, device_id=to(lax.rem(me + k, n)), device_id_type=MESH
        )

    for j in range(chips):
        fetch(j).start()
    pl.semaphore_wait(barrier, n - 1)

    cuts = cut(groups)
    halves = range(len(cuts) - 1)

    def group(h):
        return pl.ds(cuts[h], cuts[h + 1] - cuts[h])

    def remote(src, dst, sems, h, slot, peer):
        return pltpu.make_async_remote_copy(
            src_ref=src, dst_ref=dst,
            send_sem=sems.at[0, h, slot], recv_sem=sems.at[1, h, slot],
            device_id=to(peer), device_id_type=MESH,
        )

    def by_core(zz, side, h):
        j = zz * 2 + side
        return remote(
            part_ref.at[2 * j + 1 - c, group(h)], core_in.at[j, group(h)], core_sem, h, j, core_peer
        )

    def by_side(zz, h):
        return remote(
            core_in.at[zz * 2 + 1 - y, group(h)], side_in.at[zz, group(h)],
            side_sem, h, zz, side_peer,
        )

    def by_plane(zz, sign, h):
        way = 0 if sign > 0 else 1
        return remote(
            side_in.at[zz, group(h)], plane_in.at[way, zz, group(h)],
            plane_sem, h, way * planes + zz, me + 4 * sign,
        )

    def far_to_near(fn):
        for k in range(planes - 1, -1, -1):
            for h in halves:
                for sign in (1, -1):
                    zz = z + sign * k
                    @pl.when((zz >= 0) & (zz < planes))
                    def _():
                        fn(zz, k, sign, h)
                    if k == 0:
                        break

    def start_core(zz, k, sign, h):
        by_core(zz, 1 - y, h).start()
        by_core(zz, y, h).start()

    far_to_near(start_core)
    for j in range(chips):
        fetch(j).wait()

    def side_step(zz, k, sign, h):
        by_core(zz, 1 - y, h).wait_recv()
        j = zz * 2 + 1 - y
        core_in[j, group(h)] = core_in[j, group(h)] + held[j, group(h)]
        by_side(zz, h).start()

    far_to_near(side_step)

    def plane_step(zz, k, sign, h):
        by_core(zz, y, h).wait_recv()
        j = zz * 2 + y
        by_side(zz, h).wait_recv()
        total = side_in[zz, group(h)] + (core_in[j, group(h)] + held[j, group(h)])
        side_in[zz, group(h)] = total
        if k:
            behind = (z > 0) if sign > 0 else (z < planes - 1)

            @pl.when(behind)
            def _():
                by_plane(zz, sign, h).wait_recv()
                way = 0 if sign > 0 else 1
                side_in[zz, group(h)] = side_in[zz, group(h)] + plane_in[way, zz, group(h)]

            by_plane(zz, sign, h).start()

    far_to_near(plane_step)

    def by_mirror(i, g, core):
        return pltpu.make_async_remote_copy(
            src_ref=msg.at[i, core],
            dst_ref=got.at[i, c],
            send_sem=msg_sem.at[0, 2 * i + core],
            recv_sem=msg_sem.at[1, 2 * i + c],
            device_id=to(lax.rem(chip + g, chips) * 2 + core),
            device_id_type=MESH,
        )

    for h in halves:
        for ok, sign in ((z > 0, 1), (z < planes - 1, -1)):
            @pl.when(ok)
            def _():
                by_plane(z, sign, h).wait_recv()
                way = 0 if sign > 0 else 1
                side_in[z, group(h)] = side_in[z, group(h)] + plane_in[way, z, group(h)]

        for i, g in enumerate(mirrored):
            if cuts[h] <= g < cuts[h + 1]:
                for core in range(2):
                    block = side_in[z, g, :, core * tile : (core + 1) * tile]
                    msg[i, core] = jnp.concatenate([block[:half], block[half:]], axis=1)
                    by_mirror(i, g, core).start()
    for g in range(groups):
        line[lax.rem(chip + g, chips)] = side_in[z, g]
    for i, g in enumerate(mirrored):
        blocks = []
        for core in range(2):
            pltpu.make_async_remote_copy(
                src_ref=msg.at[i, core],
                dst_ref=got.at[i, core],
                send_sem=msg_sem.at[0, 2 * i + core],
                recv_sem=msg_sem.at[1, 2 * i + core],
                device_id=to(core_peer),
                device_id_type=MESH,
            ).wait_recv()
            wide = got[i, core]
            blocks.append(jnp.concatenate([wide[:, :tile], wide[:, tile:]], axis=0))
        line[lax.rem(chip + chips - g, chips)] = jnp.concatenate(blocks, axis=0).T
    columns = [line[q] for q in range(chips)]
    for q in range(chips):
        out_ref[:, q * lanes : (q + 1) * lanes] = chosen(
            columns, inv_ref[2 * q], inv_ref[2 * q + 1], tile
        )

    def sent(zz, k, sign, h):
        by_core(zz, y, h).wait_send()
        by_core(zz, 1 - y, h).wait_send()
        by_side(zz, h).wait_send()
        if k:
            by_plane(zz, sign, h).wait_send()

    far_to_near(sent)
    for i, g in enumerate(mirrored):
        for core in range(2):
            by_mirror(i, g, core).wait_send()


def shards(basis_values, basis_grads, weights, tile_lists, tile_counts, owned_rows, density_slabs):
    n = lax.axis_size("row")
    tile, width = density_slabs.shape
    npts, funcs = basis_values.shape
    planes, chips = n // 4, n // 2
    groups = chips // 2 + 1
    lanes = 2 * tile
    vmem = pl.BlockSpec(memory_space=pltpu.VMEM)
    smem = pl.BlockSpec(memory_space=pltpu.SMEM)
    dma = pltpu.SemaphoreType.DMA
    full = pl.pallas_call(
        functools.partial(gather_kernel, n),
        out_shape=jax.ShapeDtypeStruct((width, width), F32),
        in_specs=[vmem, smem],
        out_specs=vmem,
        scratch_shapes=[
            pltpu.VMEM((n, groups, tile, lanes), F32),
            dma((PIECES, 4, n)),
            dma((PIECES, n)),
        ],
        compiler_params=pltpu.CompilerParams(
            collective_id=0, has_side_effects=True, vmem_limit_bytes=VMEM_LIMIT
        ),
        name="gather_density",
    )(density_slabs, owned_rows)
    chunk = min(npts, 2**18 // funcs)
    part, inv = pl.pallas_call(
        functools.partial(compute_kernel, n, groups),
        grid=(npts // chunk,),
        out_shape=(
            jax.ShapeDtypeStruct((n, groups, tile, lanes), F32),
            jax.ShapeDtypeStruct((n,), jnp.int32),
        ),
        in_specs=[
            vmem, smem, smem, smem,
            pl.BlockSpec((chunk, funcs), lambda i: (i, 0)),
            pl.BlockSpec((3, chunk, funcs), lambda i: (0, i, 0)),
            pl.BlockSpec((1, chunk), lambda i: (0, i)),
        ],
        out_specs=(vmem, smem),
        scratch_shapes=[
            pltpu.VMEM((funcs, funcs), BF16),
            pltpu.VMEM((funcs, funcs), BF16),
            pltpu.VMEM((funcs, funcs), F32),
            pltpu.VMEM((funcs // tile, funcs, lanes), F32),
            pltpu.SMEM((n,), jnp.int32),
            pltpu.SMEM((n,), jnp.int32),
            pltpu.SMEM((n,), jnp.int32),
        ],
        compiler_params=pltpu.CompilerParams(vmem_limit_bytes=VMEM_LIMIT),
        name="batch_potential",
    )(
        full, tile_lists.T, tile_counts, owned_rows,
        basis_values, basis_grads, weights.reshape(1, npts),
    )
    mirrored = len([g for g in range(1, groups) if 2 * g != chips])
    return pl.pallas_call(
        functools.partial(reduce_kernel, n),
        out_shape=jax.ShapeDtypeStruct((tile, width), F32),
        in_specs=[pl.BlockSpec(memory_space=pl.ANY), smem],
        out_specs=vmem,
        scratch_shapes=[
            pltpu.VMEM((chips, tile, lanes), F32),
            pltpu.VMEM((chips, groups, tile, lanes), F32),
            pltpu.VMEM((planes, groups, tile, lanes), F32),
            pltpu.VMEM((2, planes, groups, tile, lanes), F32),
            pltpu.VMEM((mirrored, 2, tile // 2, lanes), F32),
            pltpu.VMEM((mirrored, 2, tile // 2, lanes), F32),
            pltpu.VMEM((chips, groups, tile, lanes), F32),
            dma((2, PIECES, chips)),
            dma((2, PIECES, planes)),
            dma((2, PIECES, 2 * planes)),
            dma((2, 2 * mirrored)),
            dma((chips,)),
        ],
        compiler_params=pltpu.CompilerParams(
            collective_id=1, has_side_effects=True, vmem_limit_bytes=VMEM_LIMIT
        ),
        name="reduce_potential",
    )(part, inv)


def solution(mesh):
    in_specs = (
        P(("parts", "row"), None),
        P(None, ("parts", "row"), None),
        P(("parts", "row")),
        P("parts", None),
        P("parts"),
        P("parts"),
        P(("parts", "row"), None),
    )
    out_specs = P(("parts", "row"), None)
    return jax.shard_map(shards, mesh=mesh, in_specs=in_specs, out_specs=out_specs, check_vma=False)
```
